512 devices in a mesh: row: 16 (over y_hi, x, core), col: 32 (over y_lo, z).
Axes of the slice: x: 4, y: 4 (y_hi: 2, y_lo: 2; y = y_hi * 2 + y_lo), z: 16, core: 2. Of those that a mesh axis runs over, the one named last changes fastest.
Arguments:
- amp_packed: float32 [6144, 3072], P('row', 'col'), may hold values from -6 to 6
- pair_rows: int32 [6144], P('row'), may hold values from 0 to 6143, as said below
- integrals: float32 [3072, 24576], P('row', 'col'), may hold values from -0.109375 to 0.109375
Outputs:
- ladder: float32 [6144, 24576], P('row', 'col')
The draws below stay inside these ranges and needn't reach their ends.
Inputs may be any that keep to these rules, and one draw needn't show every extreme that they name: `pair_rows`: A permutation of the 6144 matrix rows. Each aligned block of 384 storage positions holds exactly 24 rows of every aligned block of 384 matrix rows.
All inputs are finite; a program needn't handle non-finite values.
Results may differ from the reference program's by a relative error of at most 0.00007.
Values sent between devices are 32-bit elements; how exact they have to be, the bound alone decides.
No kernel may reach another device: no remote copies, remote signals or barrier semaphores. Data moves between devices by JAX's collectives and lax.ppermute only.
A program may use at most 64 MiB of HBM per device.

```python
import jax
import jax.numpy as jnp
from jax import lax

PAIR_DEV = 384
CD = 3072
SEND = 24
PAIRS = 6144
AB = 24576


def draw_pair_rows(key, part):
    key = jax.random.fold_in(key, 5)
    groups = PAIR_DEV // SEND
    first, second = jax.random.split(key)
    order = jax.vmap(lambda k: jax.random.permutation(k, PAIR_DEV))(jax.random.split(first, groups))
    target = order % groups
    within = order // groups
    source = jnp.arange(groups, dtype=jnp.int32)[:, None]
    shuffles = jax.vmap(lambda k: jax.random.permutation(k, PAIR_DEV))(jax.random.split(second, groups))
    place = shuffles[target, source * SEND + within]
    return (target * PAIR_DEV + place).reshape(-1).astype(jnp.int32)


def shard_levels(own_key, extent, pieces, smallest, largest):
    level, own = 1.0, jax.random.fold_in(own_key, 6)
    for dim, shards_of in pieces:
        draws = jnp.exp(jax.random.uniform(jax.random.fold_in(own, dim), (shards_of,), jnp.float32, smallest / len(pieces), largest / len(pieces)))
        level = level * jnp.repeat(draws, extent[dim] // shards_of).reshape([-1 if axis == dim else 1 for axis in range(len(extent))])
    return level


def centred(own_key, shape, deviation, limit, cuts=(), kind=jnp.bfloat16):
    drawn = jax.random.normal(own_key, shape, jnp.float32) * deviation
    if len(cuts) > 0:
        drawn = shard_levels(own_key, shape, cuts, -0.22, 0.18) * drawn
    return jnp.clip(drawn, min=-limit, max=limit).astype(kind)


def setup_inputs(seed: int = 0) -> dict:
    seeds = jax.random.split(jax.random.key(seed), 4)
    return {
        "amp_packed": centred(seeds[0], (PAIRS, CD), 1.0, 6.0, ((0, 16), (1, 32)), jnp.float32),
        "pair_rows": draw_pair_rows(jax.random.fold_in(seeds[3], 71), 0),
        "integrals": centred(seeds[2], (CD, AB), CD ** -0.5, 0.109375, ((0, 16), (1, 32)), jnp.float32),
    }


def reference(amp_packed, pair_rows, integrals):
    amp_matrix = jnp.zeros_like(amp_packed).at[pair_rows].set(amp_packed)
    return jnp.dot(amp_matrix, integrals, preferred_element_type=jnp.float32, precision=lax.Precision.HIGHEST)
```

```python
import jax
import jax.numpy as jnp
from jax import lax
from jax.experimental import pallas as pl
from jax.experimental.pallas import tpu as pltpu
from jax.sharding import Mesh, PartitionSpec as P

F32 = jnp.float32
BF16 = jnp.bfloat16
ROWS = 384
KB = 96
COLS = 768
KR = 192
CD = 3072
SEND = 24


def exact_pick(onehot, values):
    hi = values.astype(BF16)
    rest = values - hi.astype(F32)
    mid = rest.astype(BF16)
    lo = (rest - mid.astype(F32)).astype(BF16)
    dot = lambda part: jnp.dot(onehot, part, preferred_element_type=F32)
    return (dot(hi) + dot(mid)) + dot(lo)


def pack_kernel(rows_ref, own_ref, other_ref, out_ref):
    rows = rows_ref[...]
    block = ((rows >> 7) * 171) >> 9
    place = rows - block * ROWS
    down = lax.broadcasted_iota(jnp.int32, (ROWS, ROWS), 0)
    along = lax.broadcasted_iota(jnp.int32, (ROWS, ROWS), 1)
    block_f = block.astype(F32)
    diagonal = down == along
    column = lambda v: jnp.sum(jnp.where(diagonal, v, 0.0), axis=1, keepdims=True)
    same = (column(block_f) == block_f) & (down < along)
    rank = jnp.sum(jnp.where(same, 1.0, 0.0), axis=0, keepdims=True)
    position = block_f * float(SEND) + rank
    onehot = jnp.where(down.astype(F32) == position, 1.0, 0.0).astype(BF16)
    places = jnp.broadcast_to(column(place.astype(F32)), (ROWS, 32))
    values = jnp.concatenate([own_ref[...].T, places, other_ref[...].T, places], axis=1)
    out_ref[...] = exact_pick(onehot, values)


def unpack_kernel(arrived_ref, out_ref):
    arrived = arrived_ref[...]
    places = arrived[:, KB : KB + 1]
    along = lax.broadcasted_iota(jnp.int32, (ROWS, ROWS), 1).astype(F32)
    onehot = jnp.where(along == places, 1.0, 0.0).astype(BF16)
    flipped = arrived.T
    hi = flipped.astype(BF16)
    rest = flipped - hi.astype(F32)
    mid = rest.astype(BF16)
    lo = (rest - mid.astype(F32)).astype(BF16)
    dot = lambda part: jnp.dot(part, onehot, preferred_element_type=F32)
    placed = (dot(hi) + dot(mid)) + dot(lo)
    out_ref[:KB, :] = placed[:KB]
    out_ref[KB:, :] = placed[128 : 128 + KB]


def split(v):
    hi = v.astype(BF16)
    return hi, (v - hi.astype(F32)).astype(BF16)


def multiply_kernel(where_ref, amp_ref, mine_ref, twin_ref, out_ref, amp, ints, amp_sem, ints_sem):
    n_amp = 2 * 16
    core = where_ref[0]
    amp_copies = [
        pltpu.make_async_copy(
            amp_ref.at[i // 2, pl.ds((i % 2) * KB, KB), :],
            amp.at[pl.ds(pl.multiple_of(where_ref[1 + i], KB), KB), :],
            amp_sem.at[i],
        )
        for i in range(n_amp)
    ]

    def ints_copies(j):
        first = pl.multiple_of(j * 2 * KR + core * KR, KR)
        second = pl.multiple_of(j * 2 * KR + (1 - core) * KR, KR)
        return (
            pltpu.make_async_copy(mine_ref.at[j], ints.at[pl.ds(first, KR), :], ints_sem.at[0, j]),
            pltpu.make_async_copy(twin_ref.at[j], ints.at[pl.ds(second, KR), :], ints_sem.at[1, j]),
        )

    for copy in amp_copies:
        copy.start()
    for j in range(8):
        for copy in ints_copies(j):
            copy.start()
    for copy in amp_copies:
        copy.wait()
    out_ref[...] = jnp.zeros_like(out_ref)

    def step(s, carry):
        for j in range(2):
            for copy in ints_copies(s * 2 + j):
                copy.wait()
        rows = pl.ds(pl.multiple_of(s * 4 * KR, 4 * KR), 4 * KR)
        a_hi, a_lo = split(amp[rows, :].T)
        b_hi, b_lo = split(ints[rows, :])
        dot = lambda a, b: jnp.dot(a, b, preferred_element_type=F32)
        out_ref[...] += dot(a_hi, b_hi) + (dot(a_hi, b_lo) + dot(a_lo, b_hi))
        return carry

    lax.fori_loop(0, 4, step, 0)


def vmem(n):
    return [pl.BlockSpec(memory_space=pltpu.VMEM)] * n


def swap(v, axis):
    return lax.ppermute(v, axis, [(0, 1), (1, 0)])


def local(amp_packed, pair_rows, integrals):
    core, y_lo, z = lax.axis_index("core"), lax.axis_index("y_lo"), lax.axis_index("z")
    own = amp_packed.T
    other = swap(own, "y_lo")
    outgoing = pl.pallas_call(
        pack_kernel,
        out_shape=jax.ShapeDtypeStruct((ROWS, 256), F32),
        in_specs=vmem(3),
        out_specs=vmem(1)[0],
    )(pair_rows.reshape(1, ROWS), own, other)
    arrived = lax.all_to_all(outgoing, ("y_hi", "x", "core"), split_axis=0, concat_axis=0, tiled=True)
    mine = pl.pallas_call(
        unpack_kernel,
        out_shape=jax.ShapeDtypeStruct((2 * KB, ROWS), F32),
        in_specs=vmem(1),
        out_specs=vmem(1)[0],
    )(arrived)
    amp = lax.all_gather(mine, "z", axis=0, tiled=False)

    integrals, _ = lax.optimization_barrier((integrals, arrived))
    spread = jnp.broadcast_to(integrals[None], (8, KR, COLS))
    own_core = lax.all_to_all(spread, ("y_hi", "x"), split_axis=0, concat_axis=0, tiled=True)
    twin_core = swap(own_core, "core")

    zs = jnp.arange(16, dtype=jnp.int32)[:, None]
    halves = jnp.stack([y_lo, 1 - y_lo])[None, :]
    where = jnp.concatenate([core[None], (KB * (halves * 16 + zs)).reshape(-1)]).astype(jnp.int32)
    return pl.pallas_call(
        multiply_kernel,
        out_shape=jax.ShapeDtypeStruct((ROWS, COLS), F32),
        in_specs=[pl.BlockSpec(memory_space=pltpu.SMEM)] + [pl.BlockSpec(memory_space=pl.ANY)] * 3,
        out_specs=vmem(1)[0],
        scratch_shapes=[
            pltpu.VMEM((CD, ROWS), F32),
            pltpu.VMEM((CD, COLS), F32),
            pltpu.SemaphoreType.DMA((32,)),
            pltpu.SemaphoreType.DMA((2, 8)),
        ],
        compiler_params=pltpu.CompilerParams(vmem_limit_bytes=48 * 2**20),
        cost_estimate=pl.CostEstimate(flops=6 * ROWS * COLS * CD, bytes_accessed=15 * 2**20, transcendentals=0),
    )(where, amp, own_core, twin_core)


def solution(mesh):
    fine = Mesh(mesh.devices.reshape(2, 4, 2, 2, 16), ("y_hi", "x", "core", "y_lo", "z"))
    both = P(("y_hi", "x", "core"), ("y_lo", "z"))
    in_specs = (both, P(("y_hi", "x", "core")), both)
    return jax.shard_map(local, mesh=fine, in_specs=in_specs, out_specs=both, check_vma=False)
```

```python
import jax
import jax.numpy as jnp
from jax import lax
from jax.experimental import pallas as pl
from jax.experimental.pallas import tpu as pltpu
from jax.sharding import Mesh, PartitionSpec as P

F32 = jnp.float32
BF16 = jnp.bfloat16
ROWS = 384
KB = 96
COLS = 768
KR = 192
CD = 3072
SEND = 24


def exact_pick(onehot, values):
    hi = values.astype(BF16)
    rest = values - hi.astype(F32)
    mid = rest.astype(BF16)
    lo = (rest - mid.astype(F32)).astype(BF16)
    dot = lambda part: jnp.dot(onehot, part, preferred_element_type=F32)
    return (dot(hi) + dot(mid)) + dot(lo)


def pack_kernel(rows_ref, amp_ref, out_ref):
    rows = rows_ref[...].reshape(1, ROWS)
    block = ((rows >> 7) * 171) >> 9
    place = rows - block * ROWS
    down = lax.broadcasted_iota(jnp.int32, (ROWS, ROWS), 0)
    along = lax.broadcasted_iota(jnp.int32, (ROWS, ROWS), 1)
    block_f = block.astype(F32)
    diagonal = down == along
    column = lambda v: jnp.sum(jnp.where(diagonal, v, 0.0), axis=1, keepdims=True)
    same = (column(block_f) == block_f) & (down < along)
    rank = jnp.sum(jnp.where(same, 1.0, 0.0), axis=0, keepdims=True)
    position = block_f * float(SEND) + rank
    onehot = jnp.where(down.astype(F32) == position, 1.0, 0.0).astype(BF16)
    places = jnp.broadcast_to(column(place.astype(F32)), (ROWS, 128 - KB))
    values = jnp.concatenate([amp_ref[...].T, places], axis=1)
    packed = exact_pick(onehot, values)
    out_ref[:ROWS, :] = packed
    out_ref[ROWS:, :] = packed


def unpack_kernel(arrived_ref, out_ref):
    places = arrived_ref[:ROWS, KB : KB + 1]
    along = lax.broadcasted_iota(jnp.int32, (ROWS, ROWS), 1).astype(F32)
    onehot = jnp.where(along == places, 1.0, 0.0).astype(BF16)
    flipped = jnp.concatenate([arrived_ref[:ROWS, :].T[:KB], arrived_ref[ROWS:, :].T[:KB]])
    hi = flipped.astype(BF16)
    rest = flipped - hi.astype(F32)
    mid = rest.astype(BF16)
    lo = (rest - mid.astype(F32)).astype(BF16)
    dot = lambda part: jnp.dot(part, onehot, preferred_element_type=F32)
    out_ref[...] = (dot(hi) + dot(mid)) + dot(lo)


def split(v):
    hi = v.astype(BF16)
    return hi, (v - hi.astype(F32)).astype(BF16)


def multiply_kernel(core_ref, amp_ref, *refs):
    ints_refs, (out_ref, amp, amp_hi, amp_lo, sem) = refs[:2], refs[2:]
    core = core_ref[0]

    def amp_copies(i):
        which = core if i < 2 else 1 - core
        return [
            pltpu.make_async_copy(
                amp_ref.at[pl.ds(4 * j + 2 * which, 2), pl.ds(i % 2 * KB, KB), :],
                amp.at[pl.ds(8 * i + 2 * j, 2)],
                sem.at[i, j],
            )
            for j in range(4)
        ]

    for i in range(4):
        for copy in amp_copies(i):
            copy.start()
    for i in range(4):
        for copy in amp_copies(i):
            copy.wait()
        columns = slice(i * 4 * KR, (i + 1) * 4 * KR)
        amp_hi[:, columns], amp_lo[:, columns] = split(amp[8 * i : 8 * i + 8].reshape(4 * KR, ROWS).T)
    dot = lambda a, b: jnp.dot(a, b, preferred_element_type=F32)
    half = CD // 2
    for i in range(2):
        b_hi, b_lo = split(ints_refs[i][...])
        a_hi, a_lo = (ref[:, i * half : (i + 1) * half] for ref in (amp_hi, amp_lo))
        part = dot(a_hi, b_hi) + (dot(a_hi, b_lo) + dot(a_lo, b_hi))
        out_ref[...] = part if i == 0 else out_ref[...] + part


def vmem(n):
    return [pl.BlockSpec(memory_space=pltpu.VMEM)] * n


def swap(v, axis):
    return lax.ppermute(v, axis, [(0, 1), (1, 0)])


def local(amp_packed, pair_rows, integrals):
    outgoing = pl.pallas_call(
        pack_kernel,
        out_shape=jax.ShapeDtypeStruct((2 * ROWS, 128), F32),
        in_specs=vmem(2),
        out_specs=vmem(1)[0],
    )(pair_rows, amp_packed.T)
    arrived = lax.all_to_all(outgoing, ("y_lo", "y_hi", "x", "core"), split_axis=0, concat_axis=0, tiled=True)
    mine = pl.pallas_call(
        unpack_kernel,
        out_shape=jax.ShapeDtypeStruct((2 * KB, ROWS), F32),
        in_specs=vmem(1),
        out_specs=vmem(1)[0],
    )(arrived)
    amp = lax.all_gather(mine, "z", axis=0, tiled=False)

    integrals, _ = lax.optimization_barrier((integrals, arrived))
    spread = jnp.broadcast_to(integrals[None], (8, KR, COLS))
    gathered = lax.all_to_all(spread, ("y_hi", "x"), split_axis=0, concat_axis=0, tiled=True)
    twin = swap(gathered, "core")

    return pl.pallas_call(
        multiply_kernel,
        out_shape=jax.ShapeDtypeStruct((ROWS, COLS), F32),
        in_specs=[pl.BlockSpec(memory_space=pltpu.SMEM)] + [pl.BlockSpec(memory_space=pl.ANY)] + vmem(2),
        out_specs=vmem(1)[0],
        scratch_shapes=[
            pltpu.VMEM((32, KB, ROWS), F32),
            pltpu.VMEM((ROWS, CD), BF16),
            pltpu.VMEM((ROWS, CD), BF16),
            pltpu.SemaphoreType.DMA((4, 4)),
        ],
        compiler_params=pltpu.CompilerParams(vmem_limit_bytes=48 * 2**20),
        cost_estimate=pl.CostEstimate(flops=6 * ROWS * COLS * CD, bytes_accessed=15 * 2**20, transcendentals=0),
    )(lax.axis_index("core")[None], amp, gathered.reshape(CD // 2, COLS), twin.reshape(CD // 2, COLS))


def solution(mesh):
    fine = Mesh(mesh.devices.reshape(2, 4, 2, 2, 16), ("y_hi", "x", "core", "y_lo", "z"))
    both = P(("y_hi", "x", "core"), ("y_lo", "z"))
    in_specs = (both, P(("y_hi", "x", "core")), both)
    return jax.shard_map(local, mesh=fine, in_specs=in_specs, out_specs=both, check_vma=False)
```

```python
import jax
import jax.numpy as jnp
from jax import lax
from jax.experimental import pallas as pl
from jax.experimental.pallas import tpu as pltpu
from jax.sharding import Mesh, PartitionSpec as P

F32 = jnp.float32
BF16 = jnp.bfloat16
ROWS = 384
KB = 96
COLS = 768
KR = 192
CD = 3072
SEND = 24


def exact_pick(onehot, values):
    hi = values.astype(BF16)
    rest = values - hi.astype(F32)
    mid = rest.astype(BF16)
    lo = (rest - mid.astype(F32)).astype(BF16)
    dot = lambda part: jnp.dot(onehot, part, preferred_element_type=F32)
    return (dot(hi) + dot(mid)) + dot(lo)


def pack_kernel(rows_ref, amp_ref, out_ref):
    rows = rows_ref[...].reshape(1, ROWS)
    block = ((rows >> 7) * 171) >> 9
    place = rows - block * ROWS
    down = lax.broadcasted_iota(jnp.int32, (ROWS, ROWS), 0)
    along = lax.broadcasted_iota(jnp.int32, (ROWS, ROWS), 1)
    block_f = block.astype(F32)
    diagonal = down == along
    column = lambda v: jnp.sum(jnp.where(diagonal, v, 0.0), axis=1, keepdims=True)
    same = (column(block_f) == block_f) & (down < along)
    rank = jnp.sum(jnp.where(same, 1.0, 0.0), axis=0, keepdims=True)
    position = block_f * float(SEND) + rank
    onehot = jnp.where(down.astype(F32) == position, 1.0, 0.0).astype(BF16)
    places = jnp.broadcast_to(column(place.astype(F32)), (ROWS, 128 - KB))
    values = jnp.concatenate([amp_ref[...].T, places], axis=1)
    packed = exact_pick(onehot, values)
    out_ref[:ROWS, :] = packed
    out_ref[ROWS:, :] = packed


def unpack_kernel(arrived_ref, out_ref):
    places = arrived_ref[:ROWS, KB : KB + 1]
    along = lax.broadcasted_iota(jnp.int32, (ROWS, ROWS), 1).astype(F32)
    onehot = jnp.where(along == places, 1.0, 0.0).astype(BF16)
    flipped = jnp.concatenate([arrived_ref[:ROWS, :].T[:KB], arrived_ref[ROWS:, :].T[:KB]])
    hi = flipped.astype(BF16)
    rest = flipped - hi.astype(F32)
    mid = rest.astype(BF16)
    lo = (rest - mid.astype(F32)).astype(BF16)
    dot = lambda part: jnp.dot(part, onehot, preferred_element_type=F32)
    out_ref[...] = (dot(hi) + dot(mid)) + dot(lo)


def split(v):
    hi = v.astype(BF16)
    return hi, (v - hi.astype(F32)).astype(BF16)


def multiply_kernel(core_ref, amp_ref, *refs):
    ints_refs, (out_ref, amp, amp_hi, amp_lo, ints, ints_hi, ints_lo, sem, ints_sem) = refs[:2], refs[2:]
    core = core_ref[0]

    def amp_copies(i):
        which = core if i < 2 else 1 - core
        return [
            pltpu.make_async_copy(
                amp_ref.at[pl.ds(4 * j + 2 * which, 2), pl.ds(i % 2 * KB, KB), :],
                amp.at[pl.ds(8 * i + 2 * j, 2)],
                sem.at[i, j],
            )
            for j in range(4)
        ]

    def ints_copy(i):
        rows = pl.ds(i % 2 * 4 * KR, 4 * KR)
        return pltpu.make_async_copy(ints_refs[i // 2].at[rows, :], ints.at[i], ints_sem.at[i])

    for i in (0, 2):
        for copy in amp_copies(i) + amp_copies(i + 1) + [ints_copy(i), ints_copy(i + 1)]:
            copy.start()
    dot = lambda a, b: jnp.dot(a, b, preferred_element_type=F32)
    for i in range(4):
        here = slice(i * 4 * KR, (i + 1) * 4 * KR)
        for copy in amp_copies(i):
            copy.wait()
        amp_hi[:, here], amp_lo[:, here] = split(amp[8 * i : 8 * i + 8].reshape(4 * KR, ROWS).T)
        if i % 2 == 1:
            for k in (i - 1, i):
                ints_copy(k).wait()
                rows = slice(k * 4 * KR, (k + 1) * 4 * KR)
                ints_hi[rows, :], ints_lo[rows, :] = split(ints[k])
            here = slice((i - 1) * 4 * KR, (i + 1) * 4 * KR)
            a_hi, a_lo, b_hi, b_lo = amp_hi[:, here], amp_lo[:, here], ints_hi[here, :], ints_lo[here, :]
            part = dot(a_hi, b_hi) + (dot(a_hi, b_lo) + dot(a_lo, b_hi))
            out_ref[...] = part if i == 1 else out_ref[...] + part


def vmem(n):
    return [pl.BlockSpec(memory_space=pltpu.VMEM)] * n


def swap(v, axis):
    return lax.ppermute(v, axis, [(0, 1), (1, 0)])


def local(amp_packed, pair_rows, integrals):
    outgoing = pl.pallas_call(
        pack_kernel,
        out_shape=jax.ShapeDtypeStruct((2 * ROWS, 128), F32),
        in_specs=vmem(2),
        out_specs=vmem(1)[0],
    )(pair_rows, amp_packed.T)
    arrived = lax.all_to_all(outgoing, ("y_lo", "y_hi", "x", "core"), split_axis=0, concat_axis=0, tiled=True)
    mine = pl.pallas_call(
        unpack_kernel,
        out_shape=jax.ShapeDtypeStruct((2 * KB, ROWS), F32),
        in_specs=vmem(1),
        out_specs=vmem(1)[0],
    )(arrived)
    amp = lax.all_gather(mine, "z", axis=0, tiled=False)

    integrals, _ = lax.optimization_barrier((integrals, arrived))
    spread = jnp.broadcast_to(integrals[None], (8, KR, COLS))
    gathered = lax.all_to_all(spread, ("y_hi", "x"), split_axis=0, concat_axis=0, tiled=True)
    twin = swap(gathered, "core")

    return pl.pallas_call(
        multiply_kernel,
        out_shape=jax.ShapeDtypeStruct((ROWS, COLS), F32),
        in_specs=[pl.BlockSpec(memory_space=pltpu.SMEM)] + [pl.BlockSpec(memory_space=pl.ANY)] * 3,
        out_specs=vmem(1)[0],
        scratch_shapes=[
            pltpu.VMEM((32, KB, ROWS), F32),
            pltpu.VMEM((ROWS, CD), BF16),
            pltpu.VMEM((ROWS, CD), BF16),
            pltpu.VMEM((4, 4 * KR, COLS), F32),
            pltpu.VMEM((CD, COLS), BF16),
            pltpu.VMEM((CD, COLS), BF16),
            pltpu.SemaphoreType.DMA((4, 4)),
            pltpu.SemaphoreType.DMA((4,)),
        ],
        compiler_params=pltpu.CompilerParams(vmem_limit_bytes=60 * 2**20),
        cost_estimate=pl.CostEstimate(flops=6 * ROWS * COLS * CD, bytes_accessed=15 * 2**20, transcendentals=0),
    )(lax.axis_index("core")[None], amp, gathered.reshape(CD // 2, COLS), twin.reshape(CD // 2, COLS))


def solution(mesh):
    fine = Mesh(mesh.devices.reshape(2, 4, 2, 2, 16), ("y_hi", "x", "core", "y_lo", "z"))
    both = P(("y_hi", "x", "core"), ("y_lo", "z"))
    in_specs = (both, P(("y_hi", "x", "core")), both)
    return jax.shard_map(local, mesh=fine, in_specs=in_specs, out_specs=both, check_vma=False)
```

```python
import jax
import jax.numpy as jnp
from jax import lax
from jax.experimental import pallas as pl
from jax.experimental.pallas import tpu as pltpu
from jax.sharding import Mesh, PartitionSpec as P

F32 = jnp.float32
BF16 = jnp.bfloat16
ROWS = 384
KB = 96
COLS = 768
KR = 192
CD = 3072
SEND = 24


def exact_pick(onehot, values):
    hi = values.astype(BF16)
    rest = values - hi.astype(F32)
    mid = rest.astype(BF16)
    lo = (rest - mid.astype(F32)).astype(BF16)
    dot = lambda part: jnp.dot(onehot, part, preferred_element_type=F32)
    return (dot(hi) + dot(mid)) + dot(lo)


def pack_kernel(rows_ref, amp_ref, out_ref):
    rows = rows_ref[...].reshape(1, ROWS)
    block = ((rows >> 7) * 171) >> 9
    place = rows - block * ROWS
    down = lax.broadcasted_iota(jnp.int32, (ROWS, ROWS), 0)
    along = lax.broadcasted_iota(jnp.int32, (ROWS, ROWS), 1)
    block_f = block.astype(F32)
    diagonal = down == along
    column = lambda v: jnp.sum(jnp.where(diagonal, v, 0.0), axis=1, keepdims=True)
    same = (column(block_f) == block_f) & (down < along)
    rank = jnp.sum(jnp.where(same, 1.0, 0.0), axis=0, keepdims=True)
    position = block_f * float(SEND) + rank
    onehot = jnp.where(down.astype(F32) == position, 1.0, 0.0).astype(BF16)
    places = jnp.broadcast_to(column(place.astype(F32)), (ROWS, 128 - KB))
    values = jnp.concatenate([amp_ref[...].T, places], axis=1)
    packed = exact_pick(onehot, values)
    out_ref[:ROWS, :] = packed
    out_ref[ROWS:, :] = packed


def unpack_kernel(arrived_ref, out_ref):
    places = arrived_ref[:ROWS, KB : KB + 1]
    along = lax.broadcasted_iota(jnp.int32, (ROWS, ROWS), 1).astype(F32)
    onehot = jnp.where(along == places, 1.0, 0.0).astype(BF16)
    flipped = jnp.concatenate([arrived_ref[:ROWS, :].T[:KB], arrived_ref[ROWS:, :].T[:KB]])
    hi = flipped.astype(BF16)
    rest = flipped - hi.astype(F32)
    mid = rest.astype(BF16)
    lo = (rest - mid.astype(F32)).astype(BF16)
    dot = lambda part: jnp.dot(part, onehot, preferred_element_type=F32)
    out_ref[...] = (dot(hi) + dot(mid)) + dot(lo)


def split(v):
    hi = v.astype(BF16)
    return hi, (v - hi.astype(F32)).astype(BF16)


def multiply_kernel(core_ref, amp_ref, *refs):
    ints_refs, (out_ref, amp, amp_hi, amp_lo, ints, ints_hi, ints_lo, sem, ints_sem) = refs[:2], refs[2:]
    core = core_ref[0]

    def amp_copies(i):
        which = core if i < 2 else 1 - core
        return [
            pltpu.make_async_copy(
                amp_ref.at[pl.ds(4 * j + 2 * which, 2), pl.ds(i % 2 * KB, KB), :],
                amp.at[pl.ds(8 * i + 2 * j, 2)],
                sem.at[i, j],
            )
            for j in range(4)
        ]

    def ints_copy(i):
        rows = pl.ds(i % 2 * 4 * KR, 4 * KR)
        return pltpu.make_async_copy(ints_refs[i // 2].at[rows, :], ints.at[i], ints_sem.at[i])

    for i in range(4):
        for copy in [ints_copy(i)] + amp_copies(i):
            copy.start()
    for i in range(4):
        here = slice(i * 4 * KR, (i + 1) * 4 * KR)
        for copy in amp_copies(i):
            copy.wait()
        amp_hi[here, :], amp_lo[here, :] = split(amp[8 * i : 8 * i + 8].reshape(4 * KR, ROWS))
        ints_copy(i).wait()
        ints_hi[here, :], ints_lo[here, :] = split(ints[i])
    dot = lambda a, b: lax.dot_general(a[...], b[...], (((0,), (0,)), ((), ())), preferred_element_type=F32)
    out_ref[...] = dot(amp_hi, ints_hi) + (dot(amp_hi, ints_lo) + dot(amp_lo, ints_hi))


def vmem(n):
    return [pl.BlockSpec(memory_space=pltpu.VMEM)] * n


def swap(v, axis):
    return lax.ppermute(v, axis, [(0, 1), (1, 0)])


def local(amp_packed, pair_rows, integrals):
    outgoing = pl.pallas_call(
        pack_kernel,
        out_shape=jax.ShapeDtypeStruct((2 * ROWS, 128), F32),
        in_specs=vmem(2),
        out_specs=vmem(1)[0],
    )(pair_rows, amp_packed.T)
    arrived = lax.all_to_all(outgoing, ("y_lo", "y_hi", "x", "core"), split_axis=0, concat_axis=0, tiled=True)
    mine = pl.pallas_call(
        unpack_kernel,
        out_shape=jax.ShapeDtypeStruct((2 * KB, ROWS), F32),
        in_specs=vmem(1),
        out_specs=vmem(1)[0],
    )(arrived)
    amp = lax.all_gather(mine, "z", axis=0, tiled=False)

    integrals, _ = lax.optimization_barrier((integrals, arrived))
    spread = jnp.broadcast_to(integrals[None], (8, KR, COLS))
    gathered = lax.all_to_all(spread, ("y_hi", "x"), split_axis=0, concat_axis=0, tiled=True)
    twin = swap(gathered, "core")

    return pl.pallas_call(
        multiply_kernel,
        out_shape=jax.ShapeDtypeStruct((ROWS, COLS), F32),
        in_specs=[pl.BlockSpec(memory_space=pltpu.SMEM)] + [pl.BlockSpec(memory_space=pl.ANY)] * 3,
        out_specs=vmem(1)[0],
        scratch_shapes=[
            pltpu.VMEM((32, KB, ROWS), F32),
            pltpu.VMEM((CD, ROWS), BF16),
            pltpu.VMEM((CD, ROWS), BF16),
            pltpu.VMEM((4, 4 * KR, COLS), F32),
            pltpu.VMEM((CD, COLS), BF16),
            pltpu.VMEM((CD, COLS), BF16),
            pltpu.SemaphoreType.DMA((4, 4)),
            pltpu.SemaphoreType.DMA((4,)),
        ],
        compiler_params=pltpu.CompilerParams(vmem_limit_bytes=60 * 2**20),
        cost_estimate=pl.CostEstimate(flops=6 * ROWS * COLS * CD, bytes_accessed=15 * 2**20, transcendentals=0),
    )(lax.axis_index("core")[None], amp, gathered.reshape(CD // 2, COLS), twin.reshape(CD // 2, COLS))


def solution(mesh):
    fine = Mesh(mesh.devices.reshape(2, 4, 2, 2, 16), ("y_hi", "x", "core", "y_lo", "z"))
    both = P(("y_hi", "x", "core"), ("y_lo", "z"))
    in_specs = (both, P(("y_hi", "x", "core")), both)
    return jax.shard_map(local, mesh=fine, in_specs=in_specs, out_specs=both, check_vma=False)
```

```python
import jax
import jax.numpy as jnp
from jax import lax
from jax.experimental import pallas as pl
from jax.experimental.pallas import tpu as pltpu
from jax.sharding import Mesh, PartitionSpec as P

F32 = jnp.float32
BF16 = jnp.bfloat16
ROWS = 384
KB = 96
COLS = 768
KR = 192
CD = 3072
SEND = 24


def exact_dot(dot, values):
    hi = values.astype(BF16)
    rest = values - hi.astype(F32)
    mid = rest.astype(BF16)
    lo = (rest - mid.astype(F32)).astype(BF16)
    return (dot(hi) + dot(mid)) + dot(lo)


def pack_kernel(rows_ref, amp_ref, out_ref):
    rows = rows_ref[...].reshape(1, ROWS)
    block = ((rows >> 7) * 171) >> 9
    place = rows - block * ROWS
    down = lax.broadcasted_iota(jnp.int32, (ROWS, ROWS), 0)
    along = lax.broadcasted_iota(jnp.int32, (ROWS, ROWS), 1)
    block_f = block.astype(F32)
    diagonal = down == along
    column = lambda v: jnp.sum(jnp.where(diagonal, v, 0.0), axis=1, keepdims=True)
    same = (column(block_f) == block_f) & (down < along)
    rank = jnp.sum(jnp.where(same, 1.0, 0.0), axis=0, keepdims=True)
    position = block_f * float(SEND) + rank
    onehot = jnp.where(down.astype(F32) == position, 1.0, 0.0).astype(BF16)
    places = jnp.broadcast_to(place.astype(F32), (128 - KB, ROWS))
    values = jnp.concatenate([amp_ref[...], places], axis=0)
    packed = exact_dot(
        lambda part: lax.dot_general(onehot, part, (((1,), (1,)), ((), ())), preferred_element_type=F32), values
    )
    out_ref[:ROWS, :] = packed
    out_ref[ROWS:, :] = packed


def unpack_kernel(arrived_ref, out_ref):
    places = arrived_ref[:ROWS, KB : KB + 1]
    along = lax.broadcasted_iota(jnp.int32, (ROWS, ROWS), 1).astype(F32)
    onehot = jnp.where(along == places, 1.0, 0.0).astype(BF16)
    values = jnp.concatenate([arrived_ref[:ROWS, :], arrived_ref[ROWS:, :]], axis=1)
    placed = exact_dot(
        lambda part: lax.dot_general(part, onehot, (((0,), (0,)), ((), ())), preferred_element_type=F32), values
    )
    out_ref[:KB, :] = placed[:KB]
    out_ref[KB:, :] = placed[128 : 128 + KB]


def split(v):
    hi = v.astype(BF16)
    return hi, (v - hi.astype(F32)).astype(BF16)


def multiply_kernel(core_ref, amp_ref, *refs):
    ints_refs, (out_ref, amp, amp_hi, amp_lo, ints, ints_hi, ints_lo, sem, ints_sem) = refs[:2], refs[2:]
    core = core_ref[0]

    def amp_copies(i):
        which = core if i < 2 else 1 - core
        return [
            pltpu.make_async_copy(
                amp_ref.at[pl.ds(4 * j + 2 * which, 2), pl.ds(i % 2 * KB, KB), :],
                amp.at[pl.ds(8 * i + 2 * j, 2)],
                sem.at[i, j],
            )
            for j in range(4)
        ]

    def ints_copy(i):
        rows = pl.ds(i % 2 * 4 * KR, 4 * KR)
        return pltpu.make_async_copy(ints_refs[i // 2].at[rows, :], ints.at[i], ints_sem.at[i])

    for i in range(4):
        for copy in [ints_copy(i)] + amp_copies(i):
            copy.start()
    for i in range(4):
        here = slice(i * 4 * KR, (i + 1) * 4 * KR)
        for copy in amp_copies(i):
            copy.wait()
        amp_hi[here, :], amp_lo[here, :] = split(amp[8 * i : 8 * i + 8].reshape(4 * KR, ROWS))
        ints_copy(i).wait()
        ints_hi[here, :], ints_lo[here, :] = split(ints[i])
    dot = lambda a, b: lax.dot_general(a[...], b[...], (((0,), (0,)), ((), ())), preferred_element_type=F32)
    out_ref[...] = dot(amp_hi, ints_hi) + (dot(amp_hi, ints_lo) + dot(amp_lo, ints_hi))


def vmem(n):
    return [pl.BlockSpec(memory_space=pltpu.VMEM)] * n


def swap(v, axis):
    return lax.ppermute(v, axis, [(0, 1), (1, 0)])


def local(amp_packed, pair_rows, integrals):
    outgoing = pl.pallas_call(
        pack_kernel,
        out_shape=jax.ShapeDtypeStruct((2 * ROWS, 128), F32),
        in_specs=vmem(2),
        out_specs=vmem(1)[0],
    )(pair_rows, amp_packed.T)
    arrived = lax.all_to_all(outgoing, ("y_lo", "y_hi", "x", "core"), split_axis=0, concat_axis=0, tiled=True)
    mine = pl.pallas_call(
        unpack_kernel,
        out_shape=jax.ShapeDtypeStruct((2 * KB, ROWS), F32),
        in_specs=vmem(1),
        out_specs=vmem(1)[0],
    )(arrived)
    amp = lax.all_gather(mine, "z", axis=0, tiled=False)

    integrals, _ = lax.optimization_barrier((integrals, arrived))
    spread = jnp.broadcast_to(integrals[None], (8, KR, COLS))
    gathered = lax.all_to_all(spread, ("y_hi", "x"), split_axis=0, concat_axis=0, tiled=True)
    twin = swap(gathered, "core")

    return pl.pallas_call(
        multiply_kernel,
        out_shape=jax.ShapeDtypeStruct((ROWS, COLS), F32),
        in_specs=[pl.BlockSpec(memory_space=pltpu.SMEM)] + [pl.BlockSpec(memory_space=pl.ANY)] * 3,
        out_specs=vmem(1)[0],
        scratch_shapes=[
            pltpu.VMEM((32, KB, ROWS), F32),
            pltpu.VMEM((CD, ROWS), BF16),
            pltpu.VMEM((CD, ROWS), BF16),
            pltpu.VMEM((4, 4 * KR, COLS), F32),
            pltpu.VMEM((CD, COLS), BF16),
            pltpu.VMEM((CD, COLS), BF16),
            pltpu.SemaphoreType.DMA((4, 4)),
            pltpu.SemaphoreType.DMA((4,)),
        ],
        compiler_params=pltpu.CompilerParams(vmem_limit_bytes=60 * 2**20),
        cost_estimate=pl.CostEstimate(flops=6 * ROWS * COLS * CD, bytes_accessed=15 * 2**20, transcendentals=0),
    )(lax.axis_index("core")[None], amp, gathered.reshape(CD // 2, COLS), twin.reshape(CD // 2, COLS))


def solution(mesh):
    fine = Mesh(mesh.devices.reshape(2, 4, 2, 2, 16), ("y_hi", "x", "core", "y_lo", "z"))
    both = P(("y_hi", "x", "core"), ("y_lo", "z"))
    in_specs = (both, P(("y_hi", "x", "core")), both)
    return jax.shard_map(local, mesh=fine, in_specs=in_specs, out_specs=both, check_vma=False)
```

```python
import jax
import jax.numpy as jnp
from jax import lax
from jax.experimental import pallas as pl
from jax.experimental.pallas import tpu as pltpu
from jax.sharding import Mesh, PartitionSpec as P

F32 = jnp.float32
BF16 = jnp.bfloat16
ROWS = 384
KB = 96
COLS = 768
KR = 192
CD = 3072
SEND = 24


def exact_dot(dot, values):
    hi = values.astype(BF16)
    rest = values - hi.astype(F32)
    mid = rest.astype(BF16)
    lo = (rest - mid.astype(F32)).astype(BF16)
    return (dot(hi) + dot(mid)) + dot(lo)


def pack_kernel(rows_ref, amp_ref, out_ref):
    rows = rows_ref[...].reshape(1, ROWS)
    block = ((rows >> 7) * 171) >> 9
    place = rows - block * ROWS
    down = lax.broadcasted_iota(jnp.int32, (ROWS, ROWS), 0)
    along = lax.broadcasted_iota(jnp.int32, (ROWS, ROWS), 1)
    block_f = block.astype(F32)
    diagonal = down == along
    column = lambda v: jnp.sum(jnp.where(diagonal, v, 0.0), axis=1, keepdims=True)
    same = (column(block_f) == block_f) & (down < along)
    rank = jnp.sum(jnp.where(same, 1.0, 0.0), axis=0, keepdims=True)
    position = block_f * float(SEND) + rank
    onehot = jnp.where(down.astype(F32) == position, 1.0, 0.0).astype(BF16)
    places = jnp.broadcast_to(place.astype(F32), (128 - KB, ROWS))
    values = jnp.concatenate([amp_ref[...], places], axis=0)
    packed = exact_dot(
        lambda part: lax.dot_general(onehot, part, (((1,), (1,)), ((), ())), preferred_element_type=F32), values
    )
    out_ref[:ROWS, :] = packed
    out_ref[ROWS:, :] = packed


def unpack_kernel(arrived_ref, out_ref):
    places = arrived_ref[:ROWS, KB : KB + 1]
    along = lax.broadcasted_iota(jnp.int32, (ROWS, ROWS), 1).astype(F32)
    onehot = jnp.where(along == places, 1.0, 0.0).astype(BF16)
    values = jnp.concatenate([arrived_ref[:ROWS, :], arrived_ref[ROWS:, :]], axis=1)
    placed = exact_dot(
        lambda part: lax.dot_general(part, onehot, (((0,), (0,)), ((), ())), preferred_element_type=F32), values
    )
    out_ref[:KB, :] = placed[:KB]
    out_ref[KB:, :] = placed[128 : 128 + KB]


def split(v):
    hi = v.astype(BF16)
    return hi, (v - hi.astype(F32)).astype(BF16)


def multiply_kernel(core_ref, amp_ref, *refs):
    ints_refs, (out_ref, amp, amp_hi, amp_lo, ints, ints_hi, ints_lo, sem, ints_sem) = refs[:2], refs[2:]
    core = core_ref[0]

    def amp_copies(i):
        which = core if i < 2 else 1 - core
        return [
            pltpu.make_async_copy(
                amp_ref.at[pl.ds(4 * j + 2 * which, 2), pl.ds(i % 2 * KB, KB), :],
                amp.at[pl.ds(8 * i + 2 * j, 2)],
                sem.at[i, j],
            )
            for j in range(4)
        ]

    def ints_copy(i):
        rows = pl.ds(i % 2 * 4 * KR, 4 * KR)
        return pltpu.make_async_copy(ints_refs[i // 2].at[rows, :], ints.at[i], ints_sem.at[i])

    for i in range(4):
        for copy in [ints_copy(i)] + amp_copies(i):
            copy.start()
    dot = lambda a, b: lax.dot_general(a, b, (((0,), (0,)), ((), ())), preferred_element_type=F32)
    for first, last in ((0, 3), (3, 4)):
        for i in range(first, last):
            here = slice(i * 4 * KR, (i + 1) * 4 * KR)
            for copy in amp_copies(i):
                copy.wait()
            amp_hi[here, :], amp_lo[here, :] = split(amp[8 * i : 8 * i + 8].reshape(4 * KR, ROWS))
            ints_copy(i).wait()
            ints_hi[here, :], ints_lo[here, :] = split(ints[i])
        here = slice(first * 4 * KR, last * 4 * KR)
        a_hi, a_lo, b_hi, b_lo = amp_hi[here, :], amp_lo[here, :], ints_hi[here, :], ints_lo[here, :]
        part = dot(a_hi, b_hi) + (dot(a_hi, b_lo) + dot(a_lo, b_hi))
        out_ref[...] = part if first == 0 else out_ref[...] + part


def vmem(n):
    return [pl.BlockSpec(memory_space=pltpu.VMEM)] * n


def swap(v, axis):
    return lax.ppermute(v, axis, [(0, 1), (1, 0)])


def local(amp_packed, pair_rows, integrals):
    outgoing = pl.pallas_call(
        pack_kernel,
        out_shape=jax.ShapeDtypeStruct((2 * ROWS, 128), F32),
        in_specs=vmem(2),
        out_specs=vmem(1)[0],
    )(pair_rows, amp_packed.T)
    arrived = lax.all_to_all(outgoing, ("y_lo", "y_hi", "x", "core"), split_axis=0, concat_axis=0, tiled=True)
    mine = pl.pallas_call(
        unpack_kernel,
        out_shape=jax.ShapeDtypeStruct((2 * KB, ROWS), F32),
        in_specs=vmem(1),
        out_specs=vmem(1)[0],
    )(arrived)
    amp = lax.all_gather(mine, "z", axis=0, tiled=False)

    integrals, _ = lax.optimization_barrier((integrals, arrived))
    spread = jnp.broadcast_to(integrals[None], (8, KR, COLS))
    gathered = lax.all_to_all(spread, ("y_hi", "x"), split_axis=0, concat_axis=0, tiled=True)
    twin = swap(gathered, "core")

    return pl.pallas_call(
        multiply_kernel,
        out_shape=jax.ShapeDtypeStruct((ROWS, COLS), F32),
        in_specs=[pl.BlockSpec(memory_space=pltpu.SMEM)] + [pl.BlockSpec(memory_space=pl.ANY)] * 3,
        out_specs=vmem(1)[0],
        scratch_shapes=[
            pltpu.VMEM((32, KB, ROWS), F32),
            pltpu.VMEM((CD, ROWS), BF16),
            pltpu.VMEM((CD, ROWS), BF16),
            pltpu.VMEM((4, 4 * KR, COLS), F32),
            pltpu.VMEM((CD, COLS), BF16),
            pltpu.VMEM((CD, COLS), BF16),
            pltpu.SemaphoreType.DMA((4, 4)),
            pltpu.SemaphoreType.DMA((4,)),
        ],
        compiler_params=pltpu.CompilerParams(vmem_limit_bytes=60 * 2**20),
        cost_estimate=pl.CostEstimate(flops=6 * ROWS * COLS * CD, bytes_accessed=15 * 2**20, transcendentals=0),
    )(lax.axis_index("core")[None], amp, gathered.reshape(CD // 2, COLS), twin.reshape(CD // 2, COLS))


def solution(mesh):
    fine = Mesh(mesh.devices.reshape(2, 4, 2, 2, 16), ("y_hi", "x", "core", "y_lo", "z"))
    both = P(("y_hi", "x", "core"), ("y_lo", "z"))
    in_specs = (both, P(("y_hi", "x", "core")), both)
    return jax.shard_map(local, mesh=fine, in_specs=in_specs, out_specs=both, check_vma=False)
```
